32 devices in a mesh: wide: 8 (over y, x, core), narrow: 4 (over z).
Axes of the slice: x: 2, y: 2, z: 4, core: 2. Of those that a mesh axis runs over, the one named last changes fastest.
Arguments:
- start_point: int32 [32768], P(('wide', 'narrow')), may hold values from 0 to 16380
- frac_step: int32 [32768], P(('wide', 'narrow')), may hold values from 0 to 63
- targets: bfloat16 [32768], P(('wide', 'narrow')), may hold values from -6 to 6
- basis_cols: bfloat16 [16384, 2048], P(None, 'narrow'), may hold values from -0.046875 to 0.046875
Outputs:
- q_scaled: float32 [32768, 2048], P(('wide', 'narrow'))
- coefficients: float32 [2048], replicated
The draws below stay inside these ranges and needn't reach their ends.
All inputs are finite; a program needn't handle non-finite values.
Results may differ from the reference program's by a relative error of at most 0.0037.
Values may be sent and summed in bfloat16 or wider, within the bound.
No kernel may reach another device: no remote copies, remote signals or barrier semaphores. Data moves between devices by JAX's collectives and lax.ppermute only.
A program may use at most 256 MiB of HBM per device.

```python
import math
import jax
import jax.numpy as jnp
from jax import lax

K = 2048
NB = 16384
ROW_DEV = 1024
ROWS = 32768


def plant(array, stream_key, smallest, top_value):
    index_at = [jax.random.randint(jax.random.fold_in(stream_key, axis), (), 0, length) for axis, length in enumerate(array.shape)]
    longest = array.shape.index(max(array.shape))
    neighbour = index_at[:longest] + [(index_at[longest] + 1) % array.shape[longest]] + index_at[longest + 1:]
    return array.at[tuple(index_at)].set(smallest).at[tuple(neighbour)].set(top_value)


def block_levels(key, dims, shards, low, top_value):
    level = 1.0
    for axis_at, shards_of in shards:
        heights = jax.random.uniform(jax.random.fold_in(jax.random.fold_in(key, 6), axis_at), (shards_of,), jnp.float32, low / len(shards), top_value / len(shards))
        level = level * jnp.repeat(jnp.exp(heights), dims[axis_at] // shards_of).reshape((-1,) + (1,) * (len(dims) - 1 - axis_at))
    return level


def centred(stream_key, shape, width, most, split=(), held_as=jnp.bfloat16):
    values = width * jax.random.normal(stream_key, shape, jnp.float32)
    if split:
        values = values * block_levels(stream_key, shape, split, -0.22, 0.18)
    return jnp.clip(values, -most, most).astype(held_as)


def setup_inputs(seed: int = 0) -> dict:
    splits = jax.random.split(jax.random.key(seed), 5)
    start_point = plant(jax.random.randint(splits[0], (ROWS,), 0, NB - 3), jax.random.fold_in(splits[0], 1), 0, (NB - 3) - 1).astype(jnp.int32)
    frac_step = plant(jax.random.randint(splits[1], (ROWS,), 0, 64), jax.random.fold_in(splits[1], 1), 0, 63).astype(jnp.int32)
    targets = centred(splits[2], (ROWS,), 1.0, 6.0, ((0, 32),))
    basis_cols = centred(splits[3], (NB, K), (ROWS // 2) ** -0.5, 0.046875, ((1, 4),))
    return dict(start_point=start_point, frac_step=frac_step, targets=targets, basis_cols=basis_cols)


def spline_weights(frac_step):
    position = frac_step.astype(jnp.float32) / 64.0
    first = (1.0 - position) ** 3 / 6.0
    second = (3.0 * position ** 3 - 6.0 * position ** 2 + 4.0) / 6.0
    third = (-3.0 * position ** 3 + 3.0 * position ** 2 + 3.0 * position + 1.0) / 6.0
    fourth = position ** 3 / 6.0
    return [first, second, third, fourth]

def project(basis_cols, start_point, frac_step):
    weights = spline_weights(frac_step)
    accumulated = jnp.zeros((start_point.shape[0], basis_cols.shape[1]), jnp.float32)
    for offset in range(4):
        picked = jnp.take(basis_cols, start_point + offset, axis=0).astype(jnp.float32)
        accumulated = accumulated + weights[offset][:, None] * picked
    return accumulated.astype(jnp.bfloat16)

def lower_solve(chol_lower, vector, transposed):
    column = vector[:, None]
    solved = lax.linalg.triangular_solve(chol_lower, column, left_side=True, lower=True, transpose_a=transposed)
    return solved[:, 0]

def reference(start_point, frac_step, targets, basis_cols):
    block_count = ROWS // ROW_DEV
    starts_blocked = start_point.reshape(block_count, ROW_DEV)
    fracs_blocked = frac_step.reshape(block_count, ROW_DEV)

    def build_panel(contact):
        return project(basis_cols, contact[0], contact[1])
    panel_blocked = lax.map(build_panel, (starts_blocked, fracs_blocked))
    panel = panel_blocked.reshape(ROWS, K)
    gram_total = lax.dot_general(panel.astype(jnp.float32), panel.astype(jnp.float32), (((0,), (0,)), ((), ())), preferred_element_type=jnp.float32)
    chol_lower = jnp.linalg.cholesky(gram_total)

    def solve_block(block_panel):
        return lax.linalg.triangular_solve(chol_lower, block_panel.astype(jnp.float32), left_side=False, lower=True, transpose_a=True)
    q_blocked = lax.map(solve_block, panel_blocked)
    q_whole = q_blocked.reshape(ROWS, K)
    rotated = jnp.dot(targets.astype(jnp.float32), q_whole, precision=lax.Precision.HIGHEST)
    coefficients = lower_solve(chol_lower, rotated, True)
    return (q_whole * math.sqrt(ROWS), coefficients)
```

```python
import functools
import math

import jax
import jax.numpy as jnp
from jax import lax
from jax.experimental import pallas as pl
from jax.experimental.pallas import tpu as pltpu
from jax.sharding import PartitionSpec as P

VMEM = 56 * 1024 * 1024
LEAF = 128
nt = (((1,), (1,)), ((), ()))
nn = (((1,), (0,)), ((), ()))


def split(value):
    high = value.astype(jnp.bfloat16)
    low = (value - high.astype(jnp.float32)).astype(jnp.bfloat16)
    return high, low


def dot3(left, right, dims):
    def one(a, b):
        return lax.dot_general(a, b, dims, preferred_element_type=jnp.float32)

    return one(left[0], right[0]) + (one(left[0], right[1]) + one(left[1], right[0]))


def lane_spread(value, lane):
    return jnp.broadcast_to(value[:, lane : lane + 1], value.shape)


def row_spread(value, row):
    return jnp.broadcast_to(value[row : row + 1, :], value.shape)


def reciprocal(value):
    guess = pltpu.reciprocal(value, approx=True)
    return guess * (2.0 - value * guess)


def invert_leaf(m):
    size = m.shape[0]
    row_at = lax.broadcasted_iota(jnp.int32, (8, size), 0)
    lane_at = lax.broadcasted_iota(jnp.int32, (8, size), 1)
    for step in range(size // 8):
        low = 8 * step
        own = m[low : low + 8, :]
        columns = [lane_spread(own, low + j) for j in range(8)]
        inside = (lane_at >= low) & (lane_at < low + 8)
        own = jnp.where(inside, jnp.where(lane_at - low == row_at, 1.0, 0.0), own)
        pivots = jnp.ones_like(own)
        factors, inverses, rows = {}, [], []
        for j in range(8):
            pivot = row_spread(columns[j], j)
            inverse = reciprocal(pivot)
            inverses.append(inverse)
            pivots = jnp.where(row_at == j, pivot, pivots)
            rows.append(row_spread(own, j))
            if j < 7:
                scaled = jnp.where(row_at > j, columns[j] * inverse, 0.0)
                for other in range(j + 1, 8):
                    factors[j, other] = row_spread(columns[other], j)
                    columns[other] = columns[other] - scaled * factors[j, other]
                own = own - scaled * rows[j]
        for group in range(step + 1, size // 8):
            below = m[8 * group : 8 * group + 8, :]
            columns = [lane_spread(below, low + j) for j in range(8)]
            below = jnp.where(inside, 0.0, below)
            for j in range(8):
                scaled = columns[j] * inverses[j]
                for other in range(j + 1, 8):
                    columns[other] = columns[other] - scaled * factors[j, other]
                below = below - scaled * rows[j]
            m[8 * group : 8 * group + 8, :] = below
        m[low : low + 8, :] = jnp.where(lane_at < low + 8, own * lax.rsqrt(pivots), 0.0)


def invert_block(d, m):
    size = d.shape[0]
    for step in range(size // LEAF):
        low, high = step * LEAF, (step + 1) * LEAF
        m[...] = d[low:high, low:high]
        invert_leaf(m)
        leaf = split(m[...])
        pieces = [m[...]]
        if low:
            pieces.insert(0, dot3(leaf, split(d[low:high, :low]), nn))
        if high < size:
            ahead = dot3(leaf, split(d[low:high, high:]), nn)
            factor = split(dot3(split(d[high:, low:high]), leaf, nt))
            d[high:, low:high] = -dot3(factor, leaf, nn)
            d[high:, high:] = d[high:, high:] - dot3(factor, split(ahead), nn)
            if low:
                d[high:, :low] = d[high:, :low] - dot3(factor, split(pieces[0]), nn)
            pieces.append(jnp.zeros_like(ahead))
        d[low:high, :] = jnp.concatenate(pieces, axis=1)


def stage_kernel(stage, width, below, *refs):
    gram_ref = refs[0]
    earlier = [(refs[1 + 2 * k], refs[2 + 2 * k]) for k in range(stage)]
    refs = refs[1 + 2 * stage :]
    inv_high, inv_low = refs[:2]
    d, m = refs[-2:]

    def rows_of(k, first, count):
        at = pl.ds(first + (stage - k - 1) * width, count)
        return earlier[k][0][at, :], earlier[k][1][at, :]

    total = gram_ref[:width, :]
    for k in range(stage):
        own = rows_of(k, 0, width)
        total = total - dot3(own, own, nt)
    d[...] = total
    invert_block(d, m)
    high, low = split(d[...])
    inv_high[...] = high
    inv_low[...] = low
    if below:
        out_high, out_low = refs[2:4]
        tile = width // 2

        def body(index, carry):
            first = pl.multiple_of(index * tile, tile)
            value = gram_ref[pl.ds(width + first, tile), :]
            for k in range(stage):
                value = value - dot3(rows_of(k, width + first, tile), rows_of(k, 0, width), nt)
            value = dot3(split(value), (inv_high[...], inv_low[...]), nt)
            out_high[pl.ds(first, tile), :], out_low[pl.ds(first, tile), :] = split(value)
            return carry

        lax.fori_loop(0, below // tile, body, 0)


def factor_stage(stage, gram_columns, earlier):
    rows, width = gram_columns.shape
    below = rows - width
    shapes = [jax.ShapeDtypeStruct((width, width), jnp.bfloat16)] * 2
    if below:
        shapes += [jax.ShapeDtypeStruct((below, width), jnp.bfloat16)] * 2
    flat = [part for pair in earlier for part in pair]
    out = pl.pallas_call(
        functools.partial(stage_kernel, stage, width, below),
        out_shape=shapes,
        in_specs=[pl.BlockSpec(memory_space=pltpu.VMEM)] * (1 + len(flat)),
        out_specs=[pl.BlockSpec(memory_space=pltpu.VMEM)] * len(shapes),
        scratch_shapes=[pltpu.VMEM((width, width), jnp.float32), pltpu.VMEM((LEAF, LEAF), jnp.float32)],
        compiler_params=pltpu.CompilerParams(vmem_limit_bytes=VMEM),
        name="factor",
    )(gram_columns, *flat)
    return tuple(out[:2]), tuple(out[2:])


def q_kernel(count, scale, panel_ref, *refs):
    inverses = [(refs[2 * k], refs[2 * k + 1]) for k in range(count)]
    lowers = [(refs[2 * (count + k)], refs[2 * (count + k) + 1]) for k in range(count - 1)]
    out_ref = refs[-1]
    width = inverses[0][0].shape[0]
    done = []
    for stage in range(count):
        columns = slice(stage * width, (stage + 1) * width)
        inverse = (inverses[stage][0][...], inverses[stage][1][...])
        value = panel_ref[:, columns]
        if stage:
            value = value.astype(jnp.float32)
            for k in range(stage):
                at = pl.ds((stage - k - 1) * width, width)
                value = value - dot3(done[k], (lowers[k][0][at, :], lowers[k][1][at, :]), nt)
            value = dot3(split(value), inverse, nt)
        else:
            value = sum(
                lax.dot_general(value, part, nt, preferred_element_type=jnp.float32) for part in inverse[::-1]
            )
        out_ref[:, columns] = value * scale
        if stage + 1 < count:
            done.append(split(value))


def solve_panel(panel, inverses, lowers, scale):
    rows, order = panel.shape
    count = len(inverses)
    flat = [part for pair in inverses + lowers for part in pair]
    tile = min(rows, 256)
    return pl.pallas_call(
        functools.partial(q_kernel, count, scale),
        grid=(rows // tile,),
        out_shape=jax.ShapeDtypeStruct((rows, order), jnp.float32),
        in_specs=[pl.BlockSpec((tile, order), lambda i: (i, 0))]
        + [pl.BlockSpec(memory_space=pltpu.VMEM)] * len(flat),
        out_specs=pl.BlockSpec((tile, order), lambda i: (i, 0)),
        compiler_params=pltpu.CompilerParams(vmem_limit_bytes=VMEM),
        name="solve_panel",
    )(panel, *flat)


def coefficient_kernel(count, rhs_ref, *refs):
    inverses = [(refs[2 * k], refs[2 * k + 1]) for k in range(count)]
    lowers = [(refs[2 * (count + k)], refs[2 * (count + k) + 1]) for k in range(count - 1)]
    out_ref = refs[-1]
    width = inverses[0][0].shape[0]

    def lower_at(row, column):
        at = pl.ds((row - column - 1) * width, width)
        return lowers[column][0][at, :], lowers[column][1][at, :]

    def inverse_at(stage):
        return inverses[stage][0][...], inverses[stage][1][...]

    rotated = []
    for stage in range(count):
        value = rhs_ref[:, stage * width : (stage + 1) * width]
        for k in range(stage):
            value = value - dot3(rotated[k], lower_at(stage, k), nt)
        value = dot3(split(value), inverse_at(stage), nt)
        rotated.append(split(value))
    solved = {}
    for stage in reversed(range(count)):
        value = rotated[stage][0].astype(jnp.float32) + rotated[stage][1].astype(jnp.float32)
        for later in range(stage + 1, count):
            value = value - dot3(solved[later], lower_at(later, stage), nn)
        value = dot3(split(value), inverse_at(stage), nn)
        solved[stage] = split(value)
        out_ref[:, stage * width : (stage + 1) * width] = value


def solve_coefficients(rhs, inverses, lowers):
    flat = [part for pair in inverses + lowers for part in pair]
    return pl.pallas_call(
        functools.partial(coefficient_kernel, len(inverses)),
        out_shape=jax.ShapeDtypeStruct(rhs.shape, jnp.float32),
        in_specs=[pl.BlockSpec(memory_space=pltpu.VMEM)] * (1 + len(flat)),
        out_specs=pl.BlockSpec(memory_space=pltpu.VMEM),
        compiler_params=pltpu.CompilerParams(vmem_limit_bytes=VMEM),
        name="coefficients",
    )(rhs, *flat)


def spline_weights(frac_step):
    position = frac_step.astype(jnp.float32) / 64.0
    first = (1.0 - position) ** 3 / 6.0
    second = (3.0 * position**3 - 6.0 * position**2 + 4.0) / 6.0
    third = (-3.0 * position**3 + 3.0 * position**2 + 3.0 * position + 1.0) / 6.0
    fourth = position**3 / 6.0
    return [first, second, third, fourth]


def project(basis_cols, start_point, frac_step):
    weights = spline_weights(frac_step)
    accumulated = jnp.zeros((start_point.shape[0], basis_cols.shape[1]), jnp.float32)
    for offset in range(4):
        picked = jnp.take(basis_cols, start_point + offset, axis=0).astype(jnp.float32)
        accumulated = accumulated + weights[offset][:, None] * picked
    return accumulated.astype(jnp.bfloat16)


def per_device(start_point, frac_step, targets, basis_cols):
    group_start, group_frac = (
        lax.all_gather(start_point, "narrow", axis=0, tiled=True),
        lax.all_gather(frac_step, "narrow", axis=0, tiled=True),
    )
    columns = project(basis_cols, group_start, group_frac)
    panel = lax.all_to_all(columns, "narrow", split_axis=0, concat_axis=1, tiled=True)
    order = panel.shape[1]
    weighted = jnp.concatenate([panel, jnp.broadcast_to(targets[:, None], (panel.shape[0], 8))], axis=1)
    gram_local = lax.dot_general(
        weighted, panel, (((0,), (0,)), ((), ())), preferred_element_type=jnp.float32
    )
    summed = lax.psum(gram_local, ("wide", "narrow"))
    width = min(order, 512)
    inverses, lowers = [], []
    for stage in range(order // width):
        low = stage * width
        inverse, below = factor_stage(stage, summed[low:order, low : low + width], lowers)
        inverses.append(inverse)
        if below:
            lowers.append(below)
    rows_total = panel.shape[0] * lax.axis_size("wide") * lax.axis_size("narrow")
    q_scaled = solve_panel(panel, inverses, lowers, math.sqrt(rows_total))
    coefficients = solve_coefficients(summed[order:], inverses, lowers)
    return q_scaled, coefficients[0]


def solution(mesh):
    rows_at = P(("wide", "narrow"))
    return jax.shard_map(
        per_device,
        mesh=mesh,
        in_specs=(rows_at, rows_at, rows_at, P(None, "narrow")),
        out_specs=(P(("wide", "narrow"), None), P()),
        check_vma=False,
    )
```

```python
import functools
import math

import jax
import jax.numpy as jnp
from jax import lax
from jax.experimental import pallas as pl
from jax.experimental.pallas import tpu as pltpu
from jax.sharding import PartitionSpec as P

VMEM = 56 * 1024 * 1024
LEAF = 128
nt = (((1,), (1,)), ((), ()))
nn = (((1,), (0,)), ((), ()))


def split(value):
    high = value.astype(jnp.bfloat16)
    low = (value - high.astype(jnp.float32)).astype(jnp.bfloat16)
    return high, low


def dot3(left, right, dims):
    def one(a, b):
        return lax.dot_general(a, b, dims, preferred_element_type=jnp.float32)

    return one(left[0], right[0]) + (one(left[0], right[1]) + one(left[1], right[0]))


def lane_spread(value, lane):
    return jnp.broadcast_to(value[:, lane : lane + 1], value.shape)


def row_spread(value, row):
    return jnp.broadcast_to(value[row : row + 1, :], value.shape)


def reciprocal(value):
    guess = pltpu.reciprocal(value, approx=True)
    return guess * (2.0 - value * guess)


def invert_leaf(m):
    size = m.shape[0]
    row_at = lax.broadcasted_iota(jnp.int32, (8, size), 0)
    lane_at = lax.broadcasted_iota(jnp.int32, (8, size), 1)
    for step in range(size // 8):
        low = 8 * step
        own = m[low : low + 8, :]
        columns = [lane_spread(own, low + j) for j in range(8)]
        inside = (lane_at >= low) & (lane_at < low + 8)
        own = jnp.where(inside, jnp.where(lane_at - low == row_at, 1.0, 0.0), own)
        pivots = jnp.ones_like(own)
        factors, inverses, rows = {}, [], []
        for j in range(8):
            pivot = row_spread(columns[j], j)
            inverse = reciprocal(pivot)
            inverses.append(inverse)
            pivots = jnp.where(row_at == j, pivot, pivots)
            rows.append(row_spread(own, j))
            if j < 7:
                scaled = jnp.where(row_at > j, columns[j] * inverse, 0.0)
                for other in range(j + 1, 8):
                    factors[j, other] = row_spread(columns[other], j)
                    columns[other] = columns[other] - scaled * factors[j, other]
                own = own - scaled * rows[j]
        for group in range(step + 1, size // 8):
            below = m[8 * group : 8 * group + 8, :]
            columns = [lane_spread(below, low + j) for j in range(8)]
            below = jnp.where(inside, 0.0, below)
            for j in range(8):
                scaled = columns[j] * inverses[j]
                for other in range(j + 1, 8):
                    columns[other] = columns[other] - scaled * factors[j, other]
                below = below - scaled * rows[j]
            m[8 * group : 8 * group + 8, :] = below
        m[low : low + 8, :] = jnp.where(lane_at < low + 8, own * lax.rsqrt(pivots), 0.0)


def invert_block(d, m):
    size = d.shape[0]
    for step in range(size // LEAF):
        low, high = step * LEAF, (step + 1) * LEAF
        m[...] = d[low:high, low:high]
        invert_leaf(m)
        leaf = split(m[...])
        pieces = [m[...]]
        if low:
            pieces.insert(0, dot3(leaf, split(d[low:high, :low]), nn))
        if high < size:
            ahead = dot3(leaf, split(d[low:high, high:]), nn)
            factor = split(dot3(split(d[high:, low:high]), leaf, nt))
            d[high:, low:high] = -dot3(factor, leaf, nn)
            d[high:, high:] = d[high:, high:] - dot3(factor, split(ahead), nn)
            if low:
                d[high:, :low] = d[high:, :low] - dot3(factor, split(pieces[0]), nn)
            pieces.append(jnp.zeros_like(ahead))
        d[low:high, :] = jnp.concatenate(pieces, axis=1)


def read_pair(pair, first, count):
    at = pl.ds(first, count)
    return pair[0][at, :], pair[1][at, :]


def invert_kernel(stage, diag_ref, *refs):
    earlier = [(refs[2 * k], refs[2 * k + 1]) for k in range(stage)]
    inv_high, inv_low, d, m = refs[2 * stage :]
    slices, rows, width = diag_ref.shape
    count = width // slices
    for piece in range(slices):
        d[piece * count : (piece + 1) * count, :] = diag_ref[piece, :count, :]
    for k in range(stage):
        own = read_pair(earlier[k], (stage - k - 1) * width, width)
        d[...] = d[...] - dot3(own, own, nt)
    invert_block(d, m)
    inv_high[...], inv_low[...] = split(d[...])


def invert_stage(stage, diagonal, slot, earlier):
    slices, _, rows, width = diagonal.shape
    flat = [part for pair in earlier for part in pair]
    whole = pl.BlockSpec(memory_space=pltpu.VMEM)
    return pl.pallas_call(
        functools.partial(invert_kernel, stage),
        grid=(1,),
        out_shape=[jax.ShapeDtypeStruct((width, width), jnp.bfloat16)] * 2,
        in_specs=[pl.BlockSpec((slices, None, rows, width), lambda i: (0, slot, 0, 0))] + [whole] * len(flat),
        out_specs=[whole] * 2,
        scratch_shapes=[pltpu.VMEM((width, width), jnp.float32), pltpu.VMEM((LEAF, LEAF), jnp.float32)],
        compiler_params=pltpu.CompilerParams(vmem_limit_bytes=VMEM),
        cost_estimate=pl.CostEstimate(flops=25_000_000_000 if stage else 1_000_000, bytes_accessed=4 * width * width, transcendentals=0),
        name="invert_diagonal",
    )(diagonal, *flat)


def below_kernel(stage, offset, off_ref, inv_high, inv_low, *refs):
    earlier = [(refs[2 * k], refs[2 * k + 1]) for k in range(stage)]
    out_high, out_low = refs[2 * stage :]
    below, width = out_high.shape
    tile = width // 2

    def body(index, carry):
        first = pl.multiple_of(index * tile, tile)
        value = off_ref[pl.ds(offset + first, tile), :].astype(jnp.float32)
        for k in range(stage):
            skip = (stage - k - 1) * width
            value = value - dot3(
                read_pair(earlier[k], skip + width + first, tile), read_pair(earlier[k], skip, width), nt
            )
        value = dot3(split(value), (inv_high[...], inv_low[...]), nt)
        out_high[pl.ds(first, tile), :], out_low[pl.ds(first, tile), :] = split(value)
        return carry

    lax.fori_loop(0, below // tile, body, 0)


def below_stage(stage, below, off_diagonal, offset, inverse, earlier):
    width = off_diagonal.shape[1]
    flat = [part for pair in earlier for part in pair]
    whole = pl.BlockSpec(memory_space=pltpu.VMEM)
    return pl.pallas_call(
        functools.partial(below_kernel, stage, offset),
        out_shape=[jax.ShapeDtypeStruct((below, width), jnp.bfloat16)] * 2,
        in_specs=[whole] * (3 + len(flat)),
        out_specs=[whole] * 2,
        compiler_params=pltpu.CompilerParams(vmem_limit_bytes=VMEM),
        cost_estimate=pl.CostEstimate(
            flops=6 * below * width * width * (stage + 1), bytes_accessed=8 * below * width, transcendentals=0
        ),
        name="factor_below",
    )(off_diagonal, *inverse, *flat)


def q_kernel(count, scale, panel_ref, rhs_ref, *refs):
    inverses = [(refs[2 * k], refs[2 * k + 1]) for k in range(count)]
    lowers = [(refs[2 * (count + k)], refs[2 * (count + k) + 1]) for k in range(count - 1)]
    out_ref, coefficients_ref, rotated = refs[-3:]
    width = inverses[0][0].shape[0]
    rows = panel_ref.shape[0]
    done = []
    for stage in range(count):
        columns = slice(stage * width, (stage + 1) * width)
        inverse = (inverses[stage][0][...], inverses[stage][1][...])
        value = jnp.concatenate([panel_ref[:, columns].astype(jnp.float32), rhs_ref[:, columns]], axis=0)
        for k in range(stage):
            value = value - dot3(done[k], read_pair(lowers[k], (stage - k - 1) * width, width), nt)
        value = dot3(split(value), inverse, nt)
        out_ref[:, columns] = value[:rows] * scale
        rotated[:, columns] = value[rows:]
        if stage + 1 < count:
            done.append(split(value))

    @pl.when(pl.program_id(0) == 0)
    def _():
        solved = {}
        for stage in reversed(range(count)):
            columns = slice(stage * width, (stage + 1) * width)
            value = rotated[:, columns]
            for later in range(stage + 1, count):
                value = value - dot3(solved[later], read_pair(lowers[stage], (later - stage - 1) * width, width), nn)
            value = dot3(split(value), (inverses[stage][0][...], inverses[stage][1][...]), nn)
            solved[stage] = split(value)
            coefficients_ref[:, columns] = value[:1]


def solve_panel(panel, rhs, inverses, lowers, scale):
    rows, order = panel.shape
    count = len(inverses)
    flat = [part for pair in inverses + lowers for part in pair]
    tile = min(rows, 256)
    return pl.pallas_call(
        functools.partial(q_kernel, count, scale),
        grid=(rows // tile,),
        out_shape=[
            jax.ShapeDtypeStruct((rows, order), jnp.float32),
            jax.ShapeDtypeStruct((1, order), jnp.float32),
        ],
        in_specs=[pl.BlockSpec((tile, order), lambda i: (i, 0))]
        + [pl.BlockSpec(memory_space=pltpu.VMEM)] * (1 + len(flat)),
        out_specs=[pl.BlockSpec((tile, order), lambda i: (i, 0)), pl.BlockSpec((1, order), lambda i: (0, 0))],
        scratch_shapes=[pltpu.VMEM((rhs.shape[0], order), jnp.float32)],
        compiler_params=pltpu.CompilerParams(vmem_limit_bytes=VMEM),
        name="solve_panel",
    )(panel, rhs, *flat)


def spline_weights(position):
    first = (1.0 - position) ** 3 / 6.0
    second = (3.0 * position**3 - 6.0 * position**2 + 4.0) / 6.0
    third = (-3.0 * position**3 + 3.0 * position**2 + 3.0 * position + 1.0) / 6.0
    fourth = position**3 / 6.0
    return first, second, third, fourth


def gather_kernel(loads, parts, contact_ref, basis_ref, out_ref, wide_basis, weights, gathered):
    step = pl.program_id(0)
    registers = parts // 2
    together = 8 // parts
    row_at = lax.broadcasted_iota(jnp.int32, (8, 128), 0)

    @pl.when(step == 0)
    def _():
        at = lax.broadcasted_iota(jnp.int32, (8 * registers, 128), 0)
        tap = at // parts

        def fill(index, carry):
            position = (index * jnp.ones_like(at)).astype(jnp.float32) / 64.0
            first, second, third, fourth = spline_weights(position)
            value = jnp.where(tap == 0, first, jnp.where(tap == 1, second, jnp.where(tap == 2, third, fourth)))
            weights[pl.ds(pl.multiple_of(index * 8 * registers, 8), 8 * registers), :] = value
            return carry

        lax.fori_loop(0, 64, fill, 0)

    @pl.when(step < loads)
    def _():
        block = basis_ref.shape[0]
        base = step * block

        def widen(index, carry):
            first = pl.multiple_of(index * 16, 16)
            value = basis_ref[pl.ds(first, 16), :].astype(jnp.float32)
            for half in range(2):
                for part in range(parts):
                    at = (base + first + 8 * half) * parts + part
                    wide_basis[pl.ds(at, 8, stride=parts), :] = value[
                        8 * half : 8 * half + 8, 128 * part : 128 * part + 128
                    ]
            return carry

        lax.fori_loop(0, block // 16, widen, 0, unroll=4)

    @pl.when(step >= loads)
    def _():
        block = out_ref.shape[0]
        base = (step - loads) * block

        def pick(index, carry):
            value = None
            for member in range(together):
                contact = contact_ref[base + index * together + member]
                start = (contact >> 6) * parts
                frac = pl.multiple_of((contact & 63) * 8 * registers, 8)
                total = None
                for k in range(registers):
                    term = wide_basis[pl.ds(start + 8 * k, 8), :] * weights[pl.ds(frac + 8 * k, 8), :]
                    total = term if total is None else total + term
                shift = 4
                while shift >= parts:
                    total = total + pltpu.roll(total, shift, 0)
                    shift //= 2
                value = total if value is None else jnp.where(row_at >= member * parts, total, value)
            gathered[pl.ds(pl.multiple_of(index * 8, 8), 8), :] = value
            return carry

        lax.fori_loop(0, block // together, pick, 0, unroll=8)

        def narrow(index, carry):
            first = pl.multiple_of(index * 16, 16)
            pieces = []
            for part in range(parts):
                halves = [
                    gathered[pl.ds((first + 8 * half) * parts + part, 8, stride=parts), :] for half in range(2)
                ]
                pieces.append(jnp.concatenate(halves, axis=0))
            out_ref[pl.ds(first, 16), :] = jnp.concatenate(pieces, axis=1).astype(jnp.bfloat16)
            return carry

        lax.fori_loop(0, block // 16, narrow, 0, unroll=4)


def gather_columns(contact, basis_cols):
    points, columns = basis_cols.shape
    rows = contact.shape[0]
    parts = columns // 128
    in_block, out_block = 1024, 1024
    loads = points // in_block
    return pl.pallas_call(
        functools.partial(gather_kernel, loads, parts),
        grid_spec=pltpu.PrefetchScalarGridSpec(
            num_scalar_prefetch=1,
            grid=(loads + rows // out_block,),
            in_specs=[pl.BlockSpec((in_block, columns), lambda i, c: (jnp.minimum(i, loads - 1), 0))],
            out_specs=pl.BlockSpec((out_block, columns), lambda i, c: (jnp.maximum(i - loads, 0), 0)),
            scratch_shapes=[
                pltpu.VMEM((points * parts, 128), jnp.float32),
                pltpu.VMEM((64 * 4 * parts, 128), jnp.float32),
                pltpu.VMEM((out_block * parts, 128), jnp.float32),
            ],
        ),
        out_shape=jax.ShapeDtypeStruct((rows, columns), jnp.bfloat16),
        compiler_params=pltpu.CompilerParams(vmem_limit_bytes=VMEM),
        name="gather_columns",
    )(contact, basis_cols)


def piece_for(pieces, group, member, distance):
    return lax.dynamic_index_in_dim(pieces, (member + distance) % len(group(0)), 0, keepdims=False)


def shift(piece, axis, group, distance):
    pairs = []
    for device in range(lax.axis_size(axis)):
        members = group(device)
        pairs.append((device, members[(members.index(device) + distance) % len(members)]))
    return lax.ppermute(piece, axis, pairs)


def exchange(pieces, axis, group, member):
    return [
        shift(piece_for(pieces, group, member, distance), axis, group, distance)
        for distance in range(1, len(group(0)))
    ]


def spread(piece, axis, group, member, beside=None):
    size = len(group(0))
    rows = piece.shape[0]
    total = jnp.zeros((size * rows,) + piece.shape[1:], piece.dtype)
    start = (0,) * (piece.ndim - 1)
    total = lax.dynamic_update_slice(total, piece, (member * rows,) + start)
    others = [shift(piece, axis, group, distance) for distance in range(1, size)]
    if beside is not None:
        others, beside = lax.optimization_barrier((others, beside))
    for distance, other in enumerate(others, 1):
        total = lax.dynamic_update_slice(total, other, (((member - distance) % size) * rows,) + start)
    return total if beside is None else (total, beside)


def reduce_to_owner(total, axis, group, member, sent):
    size = len(group(0))
    pieces = total.reshape((size, total.shape[0] // size) + total.shape[1:])
    own = lax.dynamic_index_in_dim(pieces, member, 0, keepdims=False)
    for other in exchange(pieces.astype(sent), axis, group, member):
        own = own + other.astype(jnp.float32)
    return own


def plane_plan(wide_size):
    at = lax.axis_index("wide")
    return [
        ("wide", lambda device: [device & ~1, device | 1], at % 2),
        ("wide", lambda device: list(range(device & 1, wide_size, 2)), at // 2),
    ]


def sum_at_owner(total, plan):
    for step in plan:
        total = reduce_to_owner(total, *step, jnp.bfloat16)
    return total.astype(jnp.bfloat16)


def transposed_product(left, right):
    return lax.dot_general(left, right, (((0,), (0,)), ((), ())), preferred_element_type=jnp.float32)


def per_device(start_point, frac_step, targets, basis_cols):
    wide_size, narrow_size = lax.axis_size("wide"), lax.axis_size("narrow")
    narrow_at = lax.axis_index("narrow")
    rows, width = start_point.shape[0], basis_cols.shape[1]
    order = narrow_size * width
    plane = plane_plan(wide_size)
    line = ("narrow", lambda device: list(range(narrow_size)), narrow_at)

    contact = jnp.stack(
        [start_point.astype(jnp.float32), frac_step.astype(jnp.float32), targets.astype(jnp.float32)]
    )
    contact = lax.all_gather(contact, "narrow", axis=1, tiled=True)
    packed = contact[0].astype(jnp.int32) * 64 + contact[1].astype(jnp.int32)
    group_targets = contact[2].astype(jnp.bfloat16)
    columns = gather_columns(packed, basis_cols)

    pieces = columns.reshape(narrow_size, rows, width)
    outgoing = [piece_for(pieces, line[1], narrow_at, distance) for distance in range(1, narrow_size)]
    received = [shift(outgoing[0], *line[:2], 1)]

    square = transposed_product(columns, columns).reshape(wide_size, width // wide_size, width)
    weighted = lax.dot_general(
        jnp.broadcast_to(group_targets, (8,) + group_targets.shape),
        columns,
        (((1,), (0,)), ((), ())),
        preferred_element_type=jnp.float32,
    )
    square = jnp.concatenate([square, jnp.broadcast_to(weighted, (wide_size, 8, width))], axis=1)
    square = square.reshape(wide_size // 2, 2, -1, width).swapaxes(0, 1).reshape(wide_size, -1, width)
    for step in plane:
        square = reduce_to_owner(square, *step, jnp.float32)
    square, received = lax.optimization_barrier((square, received))
    square = spread(square, *line)
    square, outgoing = lax.optimization_barrier((square, outgoing[1:]))
    received += [shift(piece, *line[:2], distance) for distance, piece in enumerate(outgoing, 2)]
    first_square, later_squares = square[None, :1], square[None, 1:]
    for step in reversed(plane):
        first_square = spread(first_square, *step)
    for step in reversed(plane):
        later_squares = spread(later_squares, *step)
    first_square, later_squares = [
        value.reshape(2, wide_size // 2, *value.shape[1:]).swapaxes(0, 1).reshape(value.shape)
        for value in (first_square, later_squares)
    ]
    inverses = [invert_stage(0, first_square, 0, [])]
    received, inverses = lax.optimization_barrier((received, inverses))

    own = lax.dynamic_index_in_dim(pieces, narrow_at, 0, keepdims=False)
    panel = jnp.zeros((rows, order), jnp.bfloat16)
    panel = lax.dynamic_update_slice(panel, own, (0, narrow_at * width))
    for distance, piece in enumerate(received, 1):
        source = (narrow_at - distance) % narrow_size
        panel = lax.dynamic_update_slice(panel, piece, (0, source * width))

    parts = [
        transposed_product(panel[:, (stage + 1) * width :], panel[:, stage * width : (stage + 1) * width])
        for stage in range(narrow_size - 1)
    ]
    plan = plane + [line]
    off_first = sum_at_owner(parts[0], plan)
    off_later = sum_at_owner(jnp.concatenate(parts[1:], axis=0), plan)
    for step in reversed(plan):
        off_first = spread(off_first, *step)

    below = order - width
    lowers = [below_stage(0, below, off_first, 0, inverses[0], [])]
    inverses.append(invert_stage(1, later_squares, 0, lowers))
    off_later, lowers = spread(off_later, *line, lowers)
    off_later, inverses = spread(off_later, *plane[1], inverses)
    off_later = spread(off_later, *plane[0])
    offset = 0
    for stage in range(1, narrow_size):
        if stage > 1:
            inverses.append(invert_stage(stage, later_squares, stage - 1, lowers))
        below -= width
        if below:
            lowers.append(below_stage(stage, below, off_later, offset, inverses[stage], lowers))
        offset += below
    weighted = jnp.concatenate([first_square[0, :, -8:, :], later_squares[0, :, -8:, :]], axis=0)
    weighted = weighted.transpose(1, 0, 2).reshape(8, order)
    rows_total = rows * wide_size * narrow_size
    q_scaled, coefficients = solve_panel(panel, weighted, inverses, lowers, math.sqrt(rows_total))
    return q_scaled, coefficients.reshape(order)


def solution(mesh):
    rows_at = P(("wide", "narrow"))
    return jax.shard_map(
        per_device,
        mesh=mesh,
        in_specs=(rows_at, rows_at, rows_at, P(None, "narrow")),
        out_specs=(P(("wide", "narrow"), None), P()),
        check_vma=False,
    )
```

```python
import functools
import math

import jax
import jax.numpy as jnp
from jax import lax
from jax.experimental import pallas as pl
from jax.experimental.pallas import tpu as pltpu
from jax.sharding import PartitionSpec as P

VMEM = 28 * 1024 * 1024
GATHER_VMEM = 48 * 1024 * 1024
LEAF = 128
nt = (((1,), (1,)), ((), ()))
nn = (((1,), (0,)), ((), ()))


def split(value):
    high = value.astype(jnp.bfloat16)
    low = (value - high.astype(jnp.float32)).astype(jnp.bfloat16)
    return high, low


def dot3(left, right, dims):
    def one(a, b):
        return lax.dot_general(a, b, dims, preferred_element_type=jnp.float32)

    return one(left[0], right[0]) + (one(left[0], right[1]) + one(left[1], right[0]))


def lane_spread(value, lane):
    return jnp.broadcast_to(value[:, lane : lane + 1], value.shape)


def row_spread(value, row):
    return jnp.broadcast_to(value[row : row + 1, :], value.shape)


def reciprocal(value):
    guess = pltpu.reciprocal(value, approx=True)
    return guess * (2.0 - value * guess)


def invert_leaf(m):
    size = m.shape[0]
    row_at = lax.broadcasted_iota(jnp.int32, (8, size), 0)
    lane_at = lax.broadcasted_iota(jnp.int32, (8, size), 1)
    for step in range(size // 8):
        low = 8 * step
        own = m[low : low + 8, :]
        columns = [lane_spread(own, low + j) for j in range(8)]
        inside = (lane_at >= low) & (lane_at < low + 8)
        own = jnp.where(inside, jnp.where(lane_at - low == row_at, 1.0, 0.0), own)
        pivots = jnp.ones_like(own)
        factors, inverses, rows = {}, [], []
        for j in range(8):
            pivot = row_spread(columns[j], j)
            inverse = reciprocal(pivot)
            inverses.append(inverse)
            pivots = jnp.where(row_at == j, pivot, pivots)
            rows.append(row_spread(own, j))
            if j < 7:
                scaled = jnp.where(row_at > j, columns[j] * inverse, 0.0)
                for other in range(j + 1, 8):
                    factors[j, other] = row_spread(columns[other], j)
                    columns[other] = columns[other] - scaled * factors[j, other]
                own = own - scaled * rows[j]
        for group in range(step + 1, size // 8):
            below = m[8 * group : 8 * group + 8, :]
            columns = [lane_spread(below, low + j) for j in range(8)]
            below = jnp.where(inside, 0.0, below)
            for j in range(8):
                scaled = columns[j] * inverses[j]
                for other in range(j + 1, 8):
                    columns[other] = columns[other] - scaled * factors[j, other]
                below = below - scaled * rows[j]
            m[8 * group : 8 * group + 8, :] = below
        m[low : low + 8, :] = jnp.where(lane_at < low + 8, own * lax.rsqrt(pivots), 0.0)


def invert_block(d, m):
    size = d.shape[0]
    for step in range(size // LEAF):
        low, high = step * LEAF, (step + 1) * LEAF
        m[...] = d[low:high, low:high]
        invert_leaf(m)
        leaf = split(m[...])
        pieces = [m[...]]
        if low:
            pieces.insert(0, dot3(leaf, split(d[low:high, :low]), nn))
        if high < size:
            ahead = dot3(leaf, split(d[low:high, high:]), nn)
            factor = split(dot3(split(d[high:, low:high]), leaf, nt))
            d[high:, low:high] = -dot3(factor, leaf, nn)
            d[high:, high:] = d[high:, high:] - dot3(factor, split(ahead), nn)
            if low:
                d[high:, :low] = d[high:, :low] - dot3(factor, split(pieces[0]), nn)
            pieces.append(jnp.zeros_like(ahead))
        d[low:high, :] = jnp.concatenate(pieces, axis=1)


def read_pair(pair, first, count):
    at = pl.ds(first, count)
    return pair[0][at, :], pair[1][at, :]


def invert_kernel(stage, diag_ref, *refs):
    earlier = [(refs[2 * k], refs[2 * k + 1]) for k in range(stage)]
    inv_high, inv_low, d, m = refs[2 * stage :]
    slices, rows, width = diag_ref.shape
    count = width // slices
    for piece in range(slices):
        d[piece * count : (piece + 1) * count, :] = diag_ref[piece, :count, :]
    for k in range(stage):
        own = read_pair(earlier[k], (stage - k - 1) * width, width)
        d[...] = d[...] - dot3(own, own, nt)
    invert_block(d, m)
    inv_high[...], inv_low[...] = split(d[...])


def invert_stage(stage, diagonal, slot, earlier):
    slices, _, rows, width = diagonal.shape
    flat = [part for pair in earlier for part in pair]
    whole = pl.BlockSpec(memory_space=pltpu.VMEM)
    return pl.pallas_call(
        functools.partial(invert_kernel, stage),
        grid=(1,),
        out_shape=[jax.ShapeDtypeStruct((width, width), jnp.bfloat16)] * 2,
        in_specs=[pl.BlockSpec((slices, None, rows, width), lambda i: (0, slot, 0, 0))] + [whole] * len(flat),
        out_specs=[whole] * 2,
        scratch_shapes=[pltpu.VMEM((width, width), jnp.float32), pltpu.VMEM((LEAF, LEAF), jnp.float32)],
        compiler_params=pltpu.CompilerParams(vmem_limit_bytes=VMEM),
        cost_estimate=pl.CostEstimate(flops=25_000_000_000 if stage else 1_000_000, bytes_accessed=4 * width * width, transcendentals=0),
        name="invert_diagonal",
    )(diagonal, *flat)


def below_kernel(stage, offset, off_ref, inv_high, inv_low, *refs):
    earlier = [(refs[2 * k], refs[2 * k + 1]) for k in range(stage)]
    out_high, out_low = refs[2 * stage :]
    below, width = out_high.shape
    tile = width // 2

    def body(index, carry):
        first = pl.multiple_of(index * tile, tile)
        value = off_ref[pl.ds(offset + first, tile), :].astype(jnp.float32)
        for k in range(stage):
            skip = (stage - k - 1) * width
            value = value - dot3(
                read_pair(earlier[k], skip + width + first, tile), read_pair(earlier[k], skip, width), nt
            )
        value = dot3(split(value), (inv_high[...], inv_low[...]), nt)
        out_high[pl.ds(first, tile), :], out_low[pl.ds(first, tile), :] = split(value)
        return carry

    lax.fori_loop(0, below // tile, body, 0)


def below_stage(stage, below, off_diagonal, offset, inverse, earlier):
    width = off_diagonal.shape[1]
    flat = [part for pair in earlier for part in pair]
    whole = pl.BlockSpec(memory_space=pltpu.VMEM)
    return pl.pallas_call(
        functools.partial(below_kernel, stage, offset),
        out_shape=[jax.ShapeDtypeStruct((below, width), jnp.bfloat16)] * 2,
        in_specs=[whole] * (3 + len(flat)),
        out_specs=[whole] * 2,
        compiler_params=pltpu.CompilerParams(vmem_limit_bytes=VMEM),
        cost_estimate=pl.CostEstimate(
            flops=6 * below * width * width * (stage + 1), bytes_accessed=8 * below * width, transcendentals=0
        ),
        name="factor_below",
    )(off_diagonal, *inverse, *flat)


def q_kernel(count, scale, panel_ref, rhs_ref, *refs):
    inverses = [(refs[2 * k], refs[2 * k + 1]) for k in range(count)]
    lowers = [(refs[2 * (count + k)], refs[2 * (count + k) + 1]) for k in range(count - 1)]
    out_ref, coefficients_ref, rotated = refs[-3:]
    width = inverses[0][0].shape[0]
    rows = panel_ref.shape[0]
    done = []
    for stage in range(count):
        columns = slice(stage * width, (stage + 1) * width)
        inverse = (inverses[stage][0][...], inverses[stage][1][...])
        value = jnp.concatenate([panel_ref[:, columns].astype(jnp.float32), rhs_ref[:, columns]], axis=0)
        for k in range(stage):
            value = value - dot3(done[k], read_pair(lowers[k], (stage - k - 1) * width, width), nt)
        value = dot3(split(value), inverse, nt)
        out_ref[:, columns] = value[:rows] * scale
        rotated[:, columns] = value[rows:]
        if stage + 1 < count:
            done.append(split(value))

    @pl.when(pl.program_id(0) == 0)
    def _():
        solved = {}
        for stage in reversed(range(count)):
            columns = slice(stage * width, (stage + 1) * width)
            value = rotated[:, columns]
            for later in range(stage + 1, count):
                value = value - dot3(solved[later], read_pair(lowers[stage], (later - stage - 1) * width, width), nn)
            value = dot3(split(value), (inverses[stage][0][...], inverses[stage][1][...]), nn)
            solved[stage] = split(value)
            coefficients_ref[:, columns] = value[:1]


def solve_panel(panel, rhs, inverses, lowers, scale):
    rows, order = panel.shape
    count = len(inverses)
    flat = [part for pair in inverses + lowers for part in pair]
    tile = min(rows, 256)
    return pl.pallas_call(
        functools.partial(q_kernel, count, scale),
        grid=(rows // tile,),
        out_shape=[
            jax.ShapeDtypeStruct((rows, order), jnp.float32),
            jax.ShapeDtypeStruct((1, order), jnp.float32),
        ],
        in_specs=[pl.BlockSpec((tile, order), lambda i: (i, 0))]
        + [pl.BlockSpec(memory_space=pltpu.VMEM)] * (1 + len(flat)),
        out_specs=[pl.BlockSpec((tile, order), lambda i: (i, 0)), pl.BlockSpec((1, order), lambda i: (0, 0))],
        scratch_shapes=[pltpu.VMEM((rhs.shape[0], order), jnp.float32)],
        compiler_params=pltpu.CompilerParams(vmem_limit_bytes=VMEM),
        name="solve_panel",
    )(panel, rhs, *flat)


def spline_weights(position):
    first = (1.0 - position) ** 3 / 6.0
    second = (3.0 * position**3 - 6.0 * position**2 + 4.0) / 6.0
    third = (-3.0 * position**3 + 3.0 * position**2 + 3.0 * position + 1.0) / 6.0
    fourth = position**3 / 6.0
    return first, second, third, fourth


def gather_kernel(loads, parts, contact_ref, basis_ref, out_ref, wide_basis, weights, gathered):
    step = pl.program_id(0)
    registers = parts // 2
    together = 8 // parts
    row_at = lax.broadcasted_iota(jnp.int32, (8, 128), 0)

    @pl.when(step == 0)
    def _():
        at = lax.broadcasted_iota(jnp.int32, (8 * registers, 128), 0)
        tap = at // parts

        def fill(index, carry):
            position = (index * jnp.ones_like(at)).astype(jnp.float32) / 64.0
            first, second, third, fourth = spline_weights(position)
            value = jnp.where(tap == 0, first, jnp.where(tap == 1, second, jnp.where(tap == 2, third, fourth)))
            weights[pl.ds(pl.multiple_of(index * 8 * registers, 8), 8 * registers), :] = value
            return carry

        lax.fori_loop(0, 64, fill, 0)

    @pl.when(step < loads)
    def _():
        block = basis_ref.shape[0]
        base = step * block

        def widen(index, carry):
            first = pl.multiple_of(index * 16, 16)
            value = basis_ref[pl.ds(first, 16), :].astype(jnp.float32)
            for half in range(2):
                for part in range(parts):
                    at = (base + first + 8 * half) * parts + part
                    wide_basis[pl.ds(at, 8, stride=parts), :] = value[
                        8 * half : 8 * half + 8, 128 * part : 128 * part + 128
                    ]
            return carry

        lax.fori_loop(0, block // 16, widen, 0, unroll=4)

    @pl.when(step >= loads)
    def _():
        block = out_ref.shape[0]
        base = (step - loads) * block

        def pick(index, carry):
            value = None
            for member in range(together):
                contact = contact_ref[base + index * together + member]
                start = (contact >> 6) * parts
                frac = pl.multiple_of((contact & 63) * 8 * registers, 8)
                total = None
                for k in range(registers):
                    term = wide_basis[pl.ds(start + 8 * k, 8), :] * weights[pl.ds(frac + 8 * k, 8), :]
                    total = term if total is None else total + term
                shift = 4
                while shift >= parts:
                    total = total + pltpu.roll(total, shift, 0)
                    shift //= 2
                value = total if value is None else jnp.where(row_at >= member * parts, total, value)
            gathered[pl.ds(pl.multiple_of(index * 8, 8), 8), :] = value
            return carry

        lax.fori_loop(0, block // together, pick, 0, unroll=8)

        def narrow(index, carry):
            first = pl.multiple_of(index * 16, 16)
            pieces = []
            for part in range(parts):
                halves = [
                    gathered[pl.ds((first + 8 * half) * parts + part, 8, stride=parts), :] for half in range(2)
                ]
                pieces.append(jnp.concatenate(halves, axis=0))
            out_ref[pl.ds(first, 16), :] = jnp.concatenate(pieces, axis=1).astype(jnp.bfloat16)
            return carry

        lax.fori_loop(0, block // 16, narrow, 0, unroll=4)


def gather_columns(contact, basis_cols):
    points, columns = basis_cols.shape
    rows = contact.shape[0]
    parts = columns // 128
    in_block, out_block = 1024, 1024
    loads = points // in_block
    return pl.pallas_call(
        functools.partial(gather_kernel, loads, parts),
        grid_spec=pltpu.PrefetchScalarGridSpec(
            num_scalar_prefetch=1,
            grid=(loads + rows // out_block,),
            in_specs=[pl.BlockSpec((in_block, columns), lambda i, c: (jnp.minimum(i, loads - 1), 0))],
            out_specs=pl.BlockSpec((out_block, columns), lambda i, c: (jnp.maximum(i - loads, 0), 0)),
            scratch_shapes=[
                pltpu.VMEM((points * parts, 128), jnp.float32),
                pltpu.VMEM((64 * 4 * parts, 128), jnp.float32),
                pltpu.VMEM((out_block * parts, 128), jnp.float32),
            ],
        ),
        out_shape=jax.ShapeDtypeStruct((rows, columns), jnp.bfloat16),
        compiler_params=pltpu.CompilerParams(vmem_limit_bytes=GATHER_VMEM),
        name="gather_columns",
    )(contact, basis_cols)


def piece_for(pieces, group, member, distance):
    return lax.dynamic_index_in_dim(pieces, (member + distance) % len(group(0)), 0, keepdims=False)


def shift(piece, axis, group, distance):
    pairs = []
    for device in range(lax.axis_size(axis)):
        members = group(device)
        pairs.append((device, members[(members.index(device) + distance) % len(members)]))
    return lax.ppermute(piece, axis, pairs)


def exchange(pieces, axis, group, member):
    return [
        shift(piece_for(pieces, group, member, distance), axis, group, distance)
        for distance in range(1, len(group(0)))
    ]


def spread(piece, axis, group, member, beside=None):
    size = len(group(0))
    rows = piece.shape[0]
    total = jnp.zeros((size * rows,) + piece.shape[1:], piece.dtype)
    start = (0,) * (piece.ndim - 1)
    total = lax.dynamic_update_slice(total, piece, (member * rows,) + start)
    others = [shift(piece, axis, group, distance) for distance in range(1, size)]
    if beside is not None:
        others, beside = lax.optimization_barrier((others, beside))
    for distance, other in enumerate(others, 1):
        total = lax.dynamic_update_slice(total, other, (((member - distance) % size) * rows,) + start)
    return total if beside is None else (total, beside)


def reduce_to_owner(total, axis, group, member, sent):
    size = len(group(0))
    pieces = total.reshape((size, total.shape[0] // size) + total.shape[1:])
    own = lax.dynamic_index_in_dim(pieces, member, 0, keepdims=False)
    for other in exchange(pieces.astype(sent), axis, group, member):
        own = own + other.astype(jnp.float32)
    return own


def plane_plan(wide_size):
    at = lax.axis_index("wide")
    return [
        ("wide", lambda device: [device & ~1, device | 1], at % 2),
        ("wide", lambda device: list(range(device & 1, wide_size, 2)), at // 2),
    ]


def sum_at_owner(total, plan):
    for step in plan:
        total = reduce_to_owner(total, *step, jnp.bfloat16)
    return total.astype(jnp.bfloat16)


def transposed_product(left, right):
    return lax.dot_general(left, right, (((0,), (0,)), ((), ())), preferred_element_type=jnp.float32)


def per_device(start_point, frac_step, targets, basis_cols):
    wide_size, narrow_size = lax.axis_size("wide"), lax.axis_size("narrow")
    narrow_at = lax.axis_index("narrow")
    rows, width = start_point.shape[0], basis_cols.shape[1]
    order = narrow_size * width
    plane = plane_plan(wide_size)
    line = ("narrow", lambda device: list(range(narrow_size)), narrow_at)

    contact = jnp.stack(
        [start_point.astype(jnp.float32), frac_step.astype(jnp.float32), targets.astype(jnp.float32)]
    )
    contact = lax.all_gather(contact, "narrow", axis=1, tiled=True)
    packed = contact[0].astype(jnp.int32) * 64 + contact[1].astype(jnp.int32)
    group_targets = contact[2].astype(jnp.bfloat16)
    columns = gather_columns(packed, basis_cols)

    pieces = columns.reshape(narrow_size, rows, width)
    outgoing = [piece_for(pieces, line[1], narrow_at, distance) for distance in range(1, narrow_size)]
    received = [shift(outgoing[0], *line[:2], 1)]

    square = transposed_product(columns, columns).reshape(wide_size, width // wide_size, width)
    weighted = lax.dot_general(
        jnp.broadcast_to(group_targets, (8,) + group_targets.shape),
        columns,
        (((1,), (0,)), ((), ())),
        preferred_element_type=jnp.float32,
    )
    square = jnp.concatenate([square, jnp.broadcast_to(weighted, (wide_size, 8, width))], axis=1)
    square = square.reshape(wide_size // 2, 2, -1, width).swapaxes(0, 1).reshape(wide_size, -1, width)
    for step in plane:
        square = reduce_to_owner(square, *step, jnp.float32)
    square, received = lax.optimization_barrier((square, received))
    square = spread(square, *line)
    square, outgoing = lax.optimization_barrier((square, outgoing[1:]))
    received += [shift(piece, *line[:2], distance) for distance, piece in enumerate(outgoing, 2)]
    first_square, later_squares = square[None, :1], square[None, 1:]
    for step in reversed(plane):
        first_square = spread(first_square, *step)
    for step in reversed(plane):
        later_squares = spread(later_squares, *step)
    first_square, later_squares = [
        value.reshape(2, wide_size // 2, *value.shape[1:]).swapaxes(0, 1).reshape(value.shape)
        for value in (first_square, later_squares)
    ]
    inverses = [invert_stage(0, first_square, 0, [])]
    received, inverses = lax.optimization_barrier((received, inverses))

    own = lax.dynamic_index_in_dim(pieces, narrow_at, 0, keepdims=False)
    panel = jnp.zeros((rows, order), jnp.bfloat16)
    panel = lax.dynamic_update_slice(panel, own, (0, narrow_at * width))
    for distance, piece in enumerate(received, 1):
        source = (narrow_at - distance) % narrow_size
        panel = lax.dynamic_update_slice(panel, piece, (0, source * width))

    parts = [
        transposed_product(panel[:, (stage + 1) * width :], panel[:, stage * width : (stage + 1) * width])
        for stage in range(narrow_size - 1)
    ]
    plan = plane + [line]
    off_first = parts[0]
    off_later = jnp.concatenate(parts[1:], axis=0)
    for step in plane:
        off_first = reduce_to_owner(off_first, *step, jnp.bfloat16)
    off_first, off_later = lax.optimization_barrier((off_first, off_later))
    off_first = spread(sum_at_owner(off_first, [line]), *line)
    for step in plane:
        off_later = reduce_to_owner(off_later, *step, jnp.bfloat16)
    off_first, off_later = lax.optimization_barrier((off_first, off_later))
    off_later = sum_at_owner(off_later, [line])
    for step in reversed(plane):
        off_first = spread(off_first, *step)

    below = order - width
    lowers = [below_stage(0, below, off_first, 0, inverses[0], [])]
    inverses.append(invert_stage(1, later_squares, 0, lowers))
    off_later, lowers = spread(off_later, *line, lowers)
    off_later, inverses = spread(off_later, *plane[1], inverses)
    off_later = spread(off_later, *plane[0])
    offset = 0
    for stage in range(1, narrow_size):
        if stage > 1:
            inverses.append(invert_stage(stage, later_squares, stage - 1, lowers))
        below -= width
        if below:
            lowers.append(below_stage(stage, below, off_later, offset, inverses[stage], lowers))
        offset += below
    weighted = jnp.concatenate([first_square[0, :, -8:, :], later_squares[0, :, -8:, :]], axis=0)
    weighted = weighted.transpose(1, 0, 2).reshape(8, order)
    rows_total = rows * wide_size * narrow_size
    q_scaled, coefficients = solve_panel(panel, weighted, inverses, lowers, math.sqrt(rows_total))
    return q_scaled, coefficients.reshape(order)


def solution(mesh):
    rows_at = P(("wide", "narrow"))
    return jax.shard_map(
        per_device,
        mesh=mesh,
        in_specs=(rows_at, rows_at, rows_at, P(None, "narrow")),
        out_specs=(P(("wide", "narrow"), None), P()),
        check_vma=False,
    )
```
